128 devices in a mesh: col: 8 (over x_hi, y), row: 16 (over z, x_lo, core).
Axes of the slice: x: 4 (x_hi: 2, x_lo: 2; x = x_hi * 2 + x_lo), y: 4, z: 4, core: 2. Of those that a mesh axis runs over, the one named last changes fastest.
Arguments:
- corner_top_left: bfloat16 [800, 1600], P('col', 'row'), may hold values from -0.625 to 0.625
- corner_top_right: bfloat16 [800, 1600], P('col', 'row'), may hold values from -0.625 to 0.625
- corner_bottom_left: bfloat16 [800, 1600], P('col', 'row'), may hold values from -0.625 to 0.625
- edge_top: bfloat16 [800, 40000], P('col', 'row'), may hold values from -6 to 6
- edge_right: bfloat16 [800, 40000], P('col', 'row'), may hold values from -6 to 6
- edge_bottom: bfloat16 [800, 40000], P('col', 'row'), may hold values from -6 to 6
- edge_left: bfloat16 [800, 40000], P('col', 'row'), may hold values from -6 to 6
- tensors: bfloat16 [8, 625, 625], replicated, may hold values from -0.25 to 0.25
- pattern: int32 [8, 16], P('col', 'row'), may hold values from 0 to 7, as said below
- sketch_below: float32 [100, 100], replicated, may hold values from -0.4375 to 0.4375
- sketch_above: float32 [100, 100], replicated, may hold values from -0.4375 to 0.4375
- sketch_right: float32 [100, 100], replicated, may hold values from -0.4375 to 0.4375
- sketch_left: float32 [100, 100], replicated, may hold values from -0.4375 to 0.4375
Outputs:
- left_corner_top: bfloat16 [800, 1600], P('col', 'row')
- left_edge: bfloat16 [800, 40000], P('col', 'row')
- left_corner_bottom: bfloat16 [800, 1600], P('col', 'row')
- top_corner_left: bfloat16 [800, 1600], P('col', 'row')
- top_edge: bfloat16 [800, 40000], P('col', 'row')
- top_corner_right: bfloat16 [800, 1600], P('col', 'row')
The draws below stay inside these ranges and needn't reach their ends.
Inputs may be any that keep to these rules, and one draw needn't show every extreme that they name: `pattern`: each of the 8 tensors sits at exactly 16 sites.
All inputs are finite; a program needn't handle non-finite values.
Results may differ from the reference program's by a relative error of at most 0.039.
Values may be sent and summed in bfloat16 or wider, within the bound.
A program may use at most 192 MiB of HBM per device.

```python
import jax
import jax.numpy as jnp
from jax import lax

CHI = 100
DD = 25
NT = 8
LX = 8
LY = 16


def draw_pattern(key, part):
    shuffled = jax.random.permutation(jax.random.fold_in(key, 11), LX * LY)
    return (shuffled % NT).astype(jnp.int32).reshape(LX, LY)


def level_of(own_key, shape, shards, least, high):
    def one(dim, blocks):
        steps = jax.random.uniform(jax.random.fold_in(jax.random.fold_in(own_key, 6), dim), (blocks,), jnp.float32, least / len(shards), high / len(shards))
        return jnp.repeat(jnp.exp(steps), shape[dim] // blocks).reshape((-1,) + (1,) * (len(shape) - dim - 1))

    factor_of = one(*shards[0])
    for cut in shards[1:]:
        factor_of = factor_of * one(*cut)
    return factor_of


def gaussian(stream_key, shape, spread, bound, cuts=(), dtype=jnp.bfloat16):
    array = spread * jax.random.normal(stream_key, shape, jnp.float32)
    if cuts:
        array = array * level_of(stream_key, shape, cuts, -0.22, 0.18)
    return jnp.clip(array, -bound, bound).astype(dtype)


def setup_inputs(seed: int = 0) -> dict:
    seeds = jax.random.split(jax.random.key(seed), 14)
    corner_top_left = gaussian(seeds[0], (LX * CHI, LY * CHI), CHI ** -0.5, 0.625, ((0, 8), (1, 16)))
    corner_top_right = gaussian(seeds[1], (LX * CHI, LY * CHI), CHI ** -0.5, 0.625, ((0, 8), (1, 16)))
    corner_bottom_left = gaussian(seeds[2], (LX * CHI, LY * CHI), CHI ** -0.5, 0.625, ((0, 8), (1, 16)))
    edge_top = gaussian(seeds[3], (LX * CHI, LY * DD * CHI), 1.0, 6.0, ((0, 8), (1, 16)))
    edge_right = gaussian(seeds[4], (LX * CHI, LY * DD * CHI), 1.0, 6.0, ((0, 8), (1, 16)))
    edge_bottom = gaussian(seeds[5], (LX * CHI, LY * DD * CHI), 1.0, 6.0, ((0, 8), (1, 16)))
    edge_left = gaussian(seeds[6], (LX * CHI, LY * DD * CHI), 1.0, 6.0, ((0, 8), (1, 16)))
    tensors = gaussian(seeds[7], (NT, DD * DD, DD * DD), (DD * DD) ** -0.5, 0.25)
    pattern = draw_pattern(jax.random.fold_in(seeds[13], 71), 0)
    sketch_below = gaussian(seeds[9], (CHI, CHI), (2 * CHI) ** -0.5, 0.4375, (), jnp.float32)
    sketch_above = gaussian(seeds[10], (CHI, CHI), (2 * CHI) ** -0.5, 0.4375, (), jnp.float32)
    sketch_right = gaussian(seeds[11], (CHI, CHI), (2 * CHI) ** -0.5, 0.4375, (), jnp.float32)
    sketch_left = gaussian(seeds[12], (CHI, CHI), (2 * CHI) ** -0.5, 0.4375, (), jnp.float32)
    return dict(corner_top_left=corner_top_left, corner_top_right=corner_top_right, corner_bottom_left=corner_bottom_left, edge_top=edge_top, edge_right=edge_right, edge_bottom=edge_bottom, edge_left=edge_left, tensors=tensors, pattern=pattern, sketch_below=sketch_below, sketch_above=sketch_above, sketch_right=sketch_right, sketch_left=sketch_left)


def unfold_edge(edge_field):
    return edge_field.reshape(LX, CHI, LY, DD, CHI).transpose(0, 2, 1, 3, 4).astype(jnp.float32)

def fold_edge(values):
    return values.transpose(0, 2, 1, 3, 4).reshape(LX * CHI, LY * DD * CHI)

def unfold_corner(corner):
    return corner.reshape(LX, CHI, LY, CHI).transpose(0, 2, 1, 3).astype(jnp.float32)

def fold_corner(values):
    return values.transpose(0, 2, 1, 3).reshape(LX * CHI, LY * CHI)

def rms_scale(values, count):
    axes_list = tuple(range(values.ndim - count, values.ndim))
    scale = jnp.sqrt(lax.optimization_barrier(jnp.mean(values * values, axis=axes_list, keepdims=True)) + 1e-06)
    return (values / scale).astype(jnp.bfloat16)

def orthonormal(sketched):
    gram_matrix = jnp.einsum('xyra,xyrb->xyab', sketched, sketched, precision=lax.Precision.HIGHEST)
    factor = jnp.linalg.cholesky(gram_matrix)
    solved = jax.scipy.linalg.solve_triangular(factor, jnp.swapaxes(sketched, -1, -2), lower=True)
    return jnp.swapaxes(solved, -1, -2)

def sketch_with(half_field, sketch):
    return jnp.einsum('xyrc,cd->xyrd', half_field, sketch, precision=lax.Precision.HIGHEST)

def as_blocks(frame):
    return frame.astype(jnp.bfloat16).astype(jnp.float32).reshape(LX * LY, CHI, DD, CHI)

def absorb_left(operands):
    frame_in, edge_field, tensor, frame_out = operands
    mixed_rows = jnp.einsum('uip,ujd->pdij', frame_in, edge_field).astype(jnp.bfloat16)
    pushed = jnp.dot(mixed_rows.reshape(CHI * CHI, DD * DD).astype(jnp.float32), tensor.astype(jnp.float32))
    pushed = pushed.astype(jnp.bfloat16).astype(jnp.float32).reshape(CHI, CHI, DD, DD)
    return jnp.einsum('pdkr,dks->prs', pushed, frame_out)

def absorb_top(operands):
    frame_in, edge_field, tensor, frame_out = operands
    mixed_rows = jnp.einsum('ljp,lir->prij', frame_in, edge_field).astype(jnp.bfloat16)
    pushed = jnp.dot(mixed_rows.reshape(CHI * CHI, DD * DD).astype(jnp.float32), tensor.astype(jnp.float32))
    pushed = pushed.astype(jnp.bfloat16).astype(jnp.float32).reshape(CHI, CHI, DD, DD)
    return jnp.einsum('prkq,rqs->pks', pushed, frame_out)

def reference(corner_top_left, corner_top_right, corner_bottom_left, edge_top, edge_right, edge_bottom, edge_left, tensors, pattern, sketch_below, sketch_above, sketch_right, sketch_left):
    corner_one = unfold_corner(corner_top_left)
    corner_two = unfold_corner(corner_top_right)
    corner_four = unfold_corner(corner_bottom_left)
    edge_one = unfold_edge(edge_top)
    edge_two = unfold_edge(edge_right)
    edge_three = unfold_edge(edge_bottom)
    edge_four = unfold_edge(edge_left)
    site_tensors = tensors[pattern.reshape(-1)]
    upper_half = jnp.einsum('xydr,xyrkq->xydkq', corner_one, edge_one).reshape(LX, LY, CHI * DD, CHI)
    lower_half = jnp.einsum('xyur,xyrkq->xyukq', corner_four, edge_three).reshape(LX, LY, CHI * DD, CHI)
    lower_sketch = sketch_with(lower_half, sketch_below)
    upper_sketch = sketch_with(upper_half, sketch_above)
    frame_below = orthonormal(lower_sketch + jnp.roll(upper_sketch, -1, axis=1))
    frame_above = jnp.roll(frame_below, 1, axis=1)
    corner_new = rms_scale(jnp.einsum('xyap,xyaq->xypq', frame_above, upper_half, precision=lax.Precision.HIGHEST), 2)
    bottom_new = rms_scale(jnp.einsum('xyap,xyaq->xypq', frame_below, lower_half, precision=lax.Precision.HIGHEST), 2)
    edge_flat = edge_four.reshape(LX * LY, CHI, DD, CHI)
    edge_new = lax.map(absorb_left, (as_blocks(frame_above), edge_flat, site_tensors, as_blocks(frame_below)))
    edge_new = rms_scale(edge_new.reshape(LX, LY, CHI, DD, CHI), 3)
    corner_new = jnp.roll(corner_new, 1, axis=0)
    bottom_new = jnp.roll(bottom_new, 1, axis=0)
    edge_new = jnp.roll(edge_new, 1, axis=0)
    corner_next = corner_new.astype(jnp.float32)
    edge_next = edge_new.astype(jnp.float32)
    head_half = jnp.einsum('xyur,xyukw->xyrkw', corner_next, edge_next).reshape(LX, LY, CHI * DD, CHI)
    side_half = jnp.einsum('xylu,xyukd->xylkd', corner_two, edge_two).reshape(LX, LY, CHI * DD, CHI)
    side_sketch = sketch_with(side_half, sketch_right)
    head_sketch = sketch_with(head_half, sketch_left)
    frame_right = orthonormal(side_sketch + jnp.roll(head_sketch, -1, axis=0))
    frame_left = jnp.roll(frame_right, 1, axis=0)
    top_corner = rms_scale(jnp.einsum('xyaw,xyap->xywp', head_half, frame_left, precision=lax.Precision.HIGHEST), 2)
    right_corner = rms_scale(jnp.einsum('xyap,xyad->xypd', frame_right, side_half, precision=lax.Precision.HIGHEST), 2)
    top_flat = edge_one.reshape(LX * LY, CHI, DD, CHI)
    top_new = lax.map(absorb_top, (as_blocks(frame_left), top_flat, site_tensors, as_blocks(frame_right)))
    top_new = rms_scale(top_new.reshape(LX, LY, CHI, DD, CHI), 3)
    top_corner = jnp.roll(top_corner, 1, axis=1)
    right_corner = jnp.roll(right_corner, 1, axis=1)
    top_new = jnp.roll(top_new, 1, axis=1)
    return (fold_corner(corner_new), fold_edge(edge_new), fold_corner(bottom_new), fold_corner(top_corner), fold_edge(top_new), fold_corner(right_corner))
```

```python
import functools

import jax
import jax.numpy as jnp
from jax import lax
from jax.experimental import pallas as pl
from jax.experimental.pallas import tpu as pltpu
from jax.sharding import PartitionSpec as P

CHI = 100
DD = 25
LANE = 128
ROWS = 112
MAIN = DD - 1
WIDE = DD * LANE
SQUARE = 640
DEPTH = 2560
PAIRS = 13
GROUP = 4
BF = jnp.bfloat16
F32 = jnp.float32
MESH = pl.DeviceIdType.MESH


def dot(a, b):
    return jnp.dot(a, b, preferred_element_type=F32)


def dot_exact(a, b):
    return lax.dot_general(
        a, b, (((1,), (0,)), ((), ())), precision=lax.Precision.HIGHEST,
        preferred_element_type=F32,
    )


def split(values):
    high = values.astype(BF)
    return high, (values - high.astype(F32)).astype(BF)


def block(k):
    return slice(LANE * k, LANE * (k + 1))


def widen(source, target):
    target[...] = jnp.zeros_like(target)
    for k in range(DD):
        target[0:CHI, LANE * k : LANE * k + CHI] = source[:, CHI * k : CHI * (k + 1)]


def pad_square(source, target):
    target[...] = jnp.zeros_like(target)
    target[0:CHI, 0:CHI] = source[...]


def rms(values):
    scale = jnp.sqrt(jnp.sum(values * values) / (CHI * CHI) + 1e-06)
    return values / scale


def factor_inverse(gram, work):
    rows = lax.broadcasted_iota(jnp.int32, (LANE, LANE), 0)
    columns = lax.broadcasted_iota(jnp.int32, (LANE, LANE), 1)
    eye = (rows == columns).astype(F32)
    work[:, 0:LANE] = gram
    work[:, LANE:] = eye
    inner = lax.broadcasted_iota(jnp.int32, (8, 2 * LANE), 0)
    for start in range(0, 104, 8):
        panel = work[start : start + 8, :]
        for step in range(8):
            at = start + step
            if at >= CHI:
                break
            column = panel[:, at : at + 1]
            inverse = lax.rsqrt(panel[step : step + 1, at : at + 1])
            row = panel[step : step + 1, :] * inverse
            panel = jnp.where(
                inner < step,
                panel,
                jnp.where(inner == step, row, panel - (column * inverse) * row),
            )
        work[start : start + 8, :] = panel
        if start + 8 < 104:
            left = panel[:, 0:LANE]
            update = lax.dot_general(
                left, panel, (((0,), (0,)), ((), ())),
                precision=lax.Precision.HIGHEST, preferred_element_type=F32,
            )
            work[start + 8 : 104, :] = work[start + 8 : 104, :] - update[start + 8 : 104, :]
    inverse = work[:, LANE:]
    return jnp.where((rows >= CHI) & (rows != columns), 0.0, inverse)


def frame_of(sketched, others, cholesky, wide_frame, by_row, turned):
    count = len(others) + 1
    total = jnp.zeros((LANE, count * LANE), F32)
    for k in range(DD):
        own = sketched[:, block(k)]
        right = jnp.concatenate([own] + [other[:, block(k)] for other in others], axis=1)
        total = total + lax.dot_general(
            own, right, (((0,), (0,)), ((), ())), preferred_element_type=F32
        )
    rows = lax.broadcasted_iota(jnp.int32, (LANE, LANE), 0)
    columns = lax.broadcasted_iota(jnp.int32, (LANE, LANE), 1)
    gram = jnp.where((rows == columns) & (rows >= CHI), 1.0, total[:, 0:LANE])
    inverse = factor_inverse(gram, cholesky)
    products = [dot_exact(inverse, total[:, block(1 + n)]) for n in range(len(others))]
    high, low = split(inverse)
    both = jnp.concatenate([high, low], axis=0)
    for k in range(DD):
        joint = lax.dot_general(
            sketched[0:ROWS, block(k)], both, (((1,), (1,)), ((), ())),
            preferred_element_type=F32,
        )
        frame = joint[:, 0:LANE] + joint[:, LANE:]
        wide_frame[0:ROWS, block(k)] = frame.astype(BF)
        if k < MAIN:
            by_row[:, k, :] = frame[0:CHI]
        else:
            turned[:, CHI * MAIN : CHI * MAIN + ROWS] = frame.T[0:ROWS].astype(BF)
    flat = by_row[...].reshape(CHI * MAIN, LANE)
    turned[:, 0 : CHI * MAIN] = flat.T[0:ROWS].astype(BF)
    return products


def spread(edge_wide, by_row):
    for j in range(MAIN):
        by_row[:, j, :] = edge_wide[0:CHI, block(j)].astype(F32)


def absorb(by_row, edge_wide, near, arranged, rest, pushed):
    last = dot(edge_wide[0:ROWS, block(MAIN)], near[...])
    for k in range(DD):
        rest[:, k, :] = last[0:104, block(k)]

    def group(index, carry):
        first = index * GROUP
        left = by_row[pl.ds(first, GROUP)].reshape(GROUP * MAIN, LANE).astype(BF)
        mixed = dot(left, near[...])
        for pair in range(GROUP // 2):
            sides = []
            for side in range(2):
                own = 2 * pair + side
                sides.append(
                    jnp.concatenate(
                        [mixed[MAIN * own : MAIN * (own + 1), block(k)] for k in range(DD)]
                        + [rest[first + own], jnp.zeros((8, LANE), F32)],
                        axis=0,
                    ).astype(BF)
                )
            result = dot(arranged[...], jnp.concatenate(sides, axis=1))
            at = pl.multiple_of((first + 2 * pair) * MAIN, 16)
            for k in range(DD):
                rows = slice(MAIN * k, MAIN * (k + 1))
                pushed[k // 2, pl.ds(at, 2 * MAIN), block(k % 2)] = jnp.concatenate(
                    [result[rows, 0:LANE], result[rows, LANE:]], axis=0
                ).astype(BF)
            for side in range(2):
                rest[first + 2 * pair + side] = result[
                    MAIN * DD : MAIN * DD + 32, block(side)
                ]
        return carry

    lax.fori_loop(0, CHI // GROUP, group, 0)
    for k in range(DD):
        pushed[k // 2, CHI * MAIN : CHI * MAIN + ROWS, block(k % 2)] = jnp.concatenate(
            [rest[:, k, :], jnp.zeros((8, LANE), F32)], axis=0
        ).astype(BF)


def close(far, pushed, edge):
    def one(pair, total):
        value = dot(far[...], pushed[pair])
        edge[pair] = value
        return total + jnp.sum(value * value)

    total = lax.fori_loop(0, PAIRS, one, jnp.zeros((), F32))
    return jnp.sqrt(total / (CHI * DD * CHI) + 1e-06)


def narrow(edge, scale, dense, wide=None):
    for k in range(DD):
        value = (edge[k // 2, :, block(k % 2)] / scale).astype(BF)
        if wide is not None:
            wide[0:ROWS, block(k)] = value
        dense[:, CHI * k : CHI * (k + 1)] = value[0:CHI, 0:CHI]


def kernel(
    c1, c2, c4, t1, t2, t3, t4, a_left, a_top, s_below, s_above, s_right, s_left,
    o_left_top, o_left_edge, o_left_bottom, o_top_left, o_top_edge, o_top_right,
    c1_next, t1_next, far_left, far_top, corner_in,
    wide_a, wide_b, wide_c, wide_d, wide_e, wide_t, square_a, square_b,
    by_row, rest, pushed, edge, cholesky, turned, turned_top, dense, dense_top,
    corner_out, send, receive,
):
    col, row = lax.axis_index("col"), lax.axis_index("row")
    columns, rows = lax.axis_size("col"), lax.axis_size("row")
    right, left = lax.rem(col + 1, columns), lax.rem(col + columns - 1, columns)
    below, above = lax.rem(row + 1, rows), lax.rem(row + rows - 1, rows)
    to_above, to_below = (col, above), (col, below)
    to_right, to_diagonal = (right, row), (right, below)
    barrier = pltpu.get_barrier_semaphore()
    for device in (to_above, to_below, to_right, (left, row), to_diagonal, (left, above)):
        pl.semaphore_signal(barrier, inc=1, device_id=device, device_id_type=MESH)
    pl.semaphore_wait(barrier, 6)

    def ship(source, target, index, device):
        copy = pltpu.make_async_remote_copy(
            src_ref=source, dst_ref=target, send_sem=send.at[index],
            recv_sem=receive.at[index], device_id=device, device_id_type=MESH,
        )
        copy.start()
        return copy

    get_t1 = ship(t1, t1_next, 0, to_above)
    get_c1 = ship(c1, c1_next, 1, to_above)

    for ref in (wide_a, wide_b, wide_c, wide_d, wide_e):
        ref[...] = jnp.zeros_like(ref)
    rest[...] = jnp.zeros_like(rest)
    for pair in range(PAIRS):
        pushed[pair, CHI * MAIN + ROWS :, :] = jnp.zeros(
            (DEPTH - CHI * MAIN - ROWS, 2 * LANE), BF
        )
    pushed[PAIRS - 1, :, LANE:] = jnp.zeros((DEPTH, LANE), BF)
    for ref in (turned, turned_top):
        ref[:, CHI * MAIN + ROWS :] = jnp.zeros((ROWS, DEPTH - CHI * MAIN - ROWS), BF)
    widen(t2, wide_t)
    pad_square(c2, square_a)
    wide_d[0:ROWS, :] = dot(square_a[0:ROWS], wide_t[...]).astype(BF)
    widen(t3, wide_t)
    pad_square(c4, square_a)
    wide_b[0:ROWS, :] = dot(square_a[0:ROWS], wide_t[...]).astype(BF)

    def sketch_pair(sketch):
        pad_square_f32 = square_b
        pad_square_f32[...] = jnp.zeros_like(square_b)
        pad_square_f32[0:CHI, 0:CHI] = sketch[...]
        return jnp.concatenate(split(square_b[...]), axis=1)

    below_pair = sketch_pair(s_below)
    above_pair = sketch_pair(s_above)
    get_t1.wait()
    get_c1.wait()
    widen(t1_next, wide_t)
    pad_square(c1_next, square_a)
    wide_c[0:ROWS, :] = dot(square_a[0:ROWS], wide_t[...]).astype(BF)
    for k in range(DD):
        joint = dot(wide_b[0:ROWS, block(k)], below_pair) + dot(
            wide_c[0:ROWS, block(k)], above_pair
        )
        wide_a[0:ROWS, block(k)] = (joint[:, 0:LANE] + joint[:, LANE:]).astype(BF)
    bottom, top = frame_of(wide_a, (wide_b, wide_c), cholesky, wide_e, by_row, turned)
    corner_out[0] = rms(bottom)[0:CHI, 0:CHI].astype(BF)
    corner_out[1] = rms(top)[0:CHI, 0:CHI].astype(BF)
    get_far = ship(turned, far_left, 2, to_below)
    get_corner = ship(corner_out.at[1], corner_in, 3, to_below)
    put_bottom = ship(corner_out.at[0], o_left_bottom, 4, to_right)
    put_top = ship(corner_out.at[1], o_left_top, 5, to_diagonal)
    widen(t4, wide_t)
    spread(wide_t, by_row)
    absorb(by_row, wide_t, wide_e, a_left, rest, pushed)
    get_far.wait()
    scale = close(far_left, pushed, edge)
    narrow(edge, scale, dense, wide_c)
    put_edge = ship(dense, o_left_edge, 6, to_right)
    get_corner.wait()
    square_b[...] = jnp.zeros_like(square_b)
    square_b[0:CHI, 0:CHI] = corner_in[...].astype(F32)
    wide_b[0:ROWS, :] = dot(square_b[...].T[0:ROWS].astype(BF), wide_c[...]).astype(BF)
    right_pair = sketch_pair(s_right)
    left_pair = sketch_pair(s_left)
    for k in range(DD):
        joint = dot(wide_d[0:ROWS, block(k)], right_pair) + dot(
            wide_b[0:ROWS, block(k)], left_pair
        )
        wide_a[0:ROWS, block(k)] = (joint[:, 0:LANE] + joint[:, LANE:]).astype(BF)
    side, head = frame_of(wide_a, (wide_d, wide_b), cholesky, wide_e, by_row, turned_top)
    corner_out[2] = rms(side)[0:CHI, 0:CHI].astype(BF)
    corner_out[3] = rms(head).T[0:CHI, 0:CHI].astype(BF)
    get_far_top = ship(turned_top, far_top, 7, to_right)
    put_side = ship(corner_out.at[2], o_top_right, 8, to_below)
    put_head = ship(corner_out.at[3], o_top_left, 9, to_diagonal)
    widen(t1, wide_t)
    spread(wide_t, by_row)
    absorb(by_row, wide_t, wide_e, a_top, rest, pushed)
    get_far_top.wait()
    scale = close(far_top, pushed, edge)
    narrow(edge, scale, dense_top)
    put_top_edge = ship(dense_top, o_top_edge, 10, to_below)
    for copy in (put_bottom, put_top, put_edge, put_side, put_head, put_top_edge):
        copy.wait()


def arrange(tensor):
    moved = tensor.reshape(DD, DD, DD, DD).transpose(3, 0, 2, 1)
    moved = jnp.concatenate(
        [moved[:, :MAIN].reshape(DD * MAIN, DD, DD), moved[:, MAIN]], axis=0
    )
    moved = jnp.concatenate(
        [moved[:, :, :MAIN].reshape(DD * DD, DD * MAIN), moved[:, :, MAIN]], axis=1
    )
    return jnp.pad(moved, ((0, SQUARE - DD * DD), (0, SQUARE - DD * DD)))


def body(
    corner_top_left, corner_top_right, corner_bottom_left, edge_top, edge_right,
    edge_bottom, edge_left, tensors, pattern, sketch_below, sketch_above,
    sketch_right, sketch_left,
):
    tensor = lax.dynamic_index_in_dim(tensors, pattern[0, 0], 0, keepdims=False)
    arranged = arrange(tensor)
    corner = jax.ShapeDtypeStruct((CHI, CHI), BF)
    long = jax.ShapeDtypeStruct((CHI, DD * CHI), BF)
    vmem = pl.BlockSpec(memory_space=pltpu.VMEM)
    wide = pltpu.VMEM((LANE, WIDE), BF)
    return pl.pallas_call(
        kernel,
        out_shape=(corner, long, corner, corner, long, corner),
        in_specs=[vmem] * 13,
        out_specs=[pl.BlockSpec(memory_space=pl.ANY)] * 6,
        scratch_shapes=[
            pltpu.VMEM((CHI, CHI), BF),
            pltpu.VMEM((CHI, DD * CHI), BF),
            pltpu.VMEM((ROWS, DEPTH), BF),
            pltpu.VMEM((ROWS, DEPTH), BF),
            pltpu.VMEM((CHI, CHI), BF),
            wide, wide, wide, wide, wide, wide,
            pltpu.VMEM((LANE, LANE), BF),
            pltpu.VMEM((LANE, LANE), F32),
            pltpu.VMEM((CHI, MAIN, LANE), F32),
            pltpu.VMEM((104, 32, LANE), F32),
            pltpu.VMEM((PAIRS, DEPTH, 2 * LANE), BF),
            pltpu.VMEM((PAIRS, ROWS, 2 * LANE), F32),
            pltpu.VMEM((LANE, 2 * LANE), F32),
            pltpu.VMEM((ROWS, DEPTH), BF),
            pltpu.VMEM((ROWS, DEPTH), BF),
            pltpu.VMEM((CHI, DD * CHI), BF),
            pltpu.VMEM((CHI, DD * CHI), BF),
            pltpu.VMEM((4, CHI, CHI), BF),
            pltpu.SemaphoreType.DMA((11,)),
            pltpu.SemaphoreType.DMA((11,)),
        ],
        compiler_params=pltpu.CompilerParams(
            collective_id=0, has_side_effects=True, vmem_limit_bytes=60 * 1024 * 1024
        ),
    )(
        corner_top_left, corner_top_right, corner_bottom_left, edge_top, edge_right,
        edge_bottom, edge_left, arranged, arranged.T, sketch_below, sketch_above,
        sketch_right, sketch_left,
    )


def solution(mesh):
    split_both = P("col", "row")
    in_specs = (split_both,) * 7 + (P(), split_both) + (P(),) * 4
    return jax.shard_map(
        body, mesh=mesh, in_specs=in_specs, out_specs=(split_both,) * 6, check_vma=False
    )
```

```python
import functools

import jax
import jax.numpy as jnp
from jax import lax
from jax.experimental import pallas as pl
from jax.experimental.pallas import tpu as pltpu
from jax.sharding import PartitionSpec as P

CHI = 100
DD = 25
LANE = 128
ROWS = 112
MAIN = DD - 1
WIDE = DD * LANE
SQUARE = 640
DEPTH = 2560
PAIRS = 13
GROUP = 20
BATCH = 2
BF = jnp.bfloat16
F32 = jnp.float32
MESH = pl.DeviceIdType.MESH


def dot(a, b):
    return jnp.dot(a, b, preferred_element_type=F32)


def dot_exact(a, b):
    return lax.dot_general(
        a, b, (((1,), (0,)), ((), ())), precision=lax.Precision.HIGHEST,
        preferred_element_type=F32,
    )


def split(values):
    high = values.astype(BF)
    return high, (values - high.astype(F32)).astype(BF)


def block(k):
    return slice(LANE * k, LANE * (k + 1))


def widen(source, target):
    target[...] = jnp.zeros_like(target)
    for k in range(DD):
        target[0:CHI, LANE * k : LANE * k + CHI] = source[:, CHI * k : CHI * (k + 1)]


def pad_square(source, target):
    target[...] = jnp.zeros_like(target)
    target[0:CHI, 0:CHI] = source[...]


def rms(values):
    scale = jnp.sqrt(jnp.sum(values * values) / (CHI * CHI) + 1e-06)
    return values / scale


def factor_inverse(gram, work):
    rows = lax.broadcasted_iota(jnp.int32, (LANE, LANE), 0)
    columns = lax.broadcasted_iota(jnp.int32, (LANE, LANE), 1)
    eye = (rows == columns).astype(F32)
    work[:, 0:LANE] = gram
    work[:, LANE:] = eye
    inner = lax.broadcasted_iota(jnp.int32, (8, LANE), 0)
    for start in range(0, 104, 8):
        halves = [work[start : start + 8, block(n)] for n in range(2)]
        tall = [
            jnp.broadcast_to(halves[0][:, start + n : start + n + 1], (8, LANE)) for n in range(8)
        ]
        for step in range(8):
            if start + step >= CHI:
                break
            inverse = lax.rsqrt(jnp.broadcast_to(tall[step][step : step + 1], (8, LANE)))
            factor = tall[step] * inverse
            for later in range(step + 1, 8):
                tall[later] = tall[later] - factor * factor[later : later + 1]
            for n in range(2):
                row = halves[n][step : step + 1] * inverse
                halves[n] = jnp.where(
                    inner < step,
                    halves[n],
                    jnp.where(inner == step, row, halves[n] - factor * row),
                )
        panel = jnp.concatenate(halves, axis=1)
        work[start : start + 8, :] = panel
        if start + 8 < 104:
            high = panel.astype(BF).astype(F32)
            middle = (panel - high).astype(BF).astype(F32)
            low = panel - high - middle
            tall_parts = [part[:, :LANE] for part in (high, high, high, middle, middle, low)]
            update = lax.dot_general(
                jnp.concatenate(tall_parts, axis=0).T.astype(BF),
                jnp.concatenate([high, middle, low, high, middle, high], axis=0).astype(BF),
                (((1,), (0,)), ((), ())), preferred_element_type=F32,
            )
            work[start + 8 : 104, :] = work[start + 8 : 104, :] - update[start + 8 : 104, :]
    inverse = work[:, LANE:]
    return jnp.where((rows >= CHI) & (rows != columns), 0.0, inverse)


def frame_of(sketched, others, cholesky, wide_frame, by_row, turned):
    count = len(others) + 1
    total = jnp.zeros((LANE, count * LANE), F32)
    for k in range(DD):
        own = sketched[:, block(k)]
        right = jnp.concatenate([own] + [other[:, block(k)] for other in others], axis=1)
        total = total + lax.dot_general(
            own, right, (((0,), (0,)), ((), ())), preferred_element_type=F32
        )
    rows = lax.broadcasted_iota(jnp.int32, (LANE, LANE), 0)
    columns = lax.broadcasted_iota(jnp.int32, (LANE, LANE), 1)
    gram = jnp.where((rows == columns) & (rows >= CHI), 1.0, total[:, 0:LANE])
    inverse = factor_inverse(gram, cholesky)
    products = [dot_exact(inverse, total[:, block(1 + n)]) for n in range(len(others))]
    high, low = split(inverse)
    both = jnp.concatenate([high, low], axis=0)
    for k in range(DD):
        joint = lax.dot_general(
            sketched[0:ROWS, block(k)], both, (((1,), (1,)), ((), ())),
            preferred_element_type=F32,
        )
        frame = joint[:, 0:LANE] + joint[:, LANE:]
        wide_frame[0:ROWS, block(k)] = frame.astype(BF)
        if k < MAIN:
            by_row[:, k, :] = frame[0:CHI]
        else:
            turned[:, CHI * MAIN : CHI * MAIN + ROWS] = frame.T[0:ROWS].astype(BF)
    flat = by_row[...].reshape(CHI * MAIN, LANE)
    turned[:, 0 : CHI * MAIN] = flat.T[0:ROWS].astype(BF)
    return products


def spread(edge_wide, by_row):
    for j in range(MAIN):
        by_row[:, j, :] = edge_wide[0:CHI, block(j)].astype(F32)


def absorb(by_row, edge_wide, near, arranged, rest, pushed):
    last = dot(edge_wide[0:ROWS, block(MAIN)], near[...])
    for k in range(DD):
        rest[:, k, :] = last[0:104, block(k)]

    def group(index, carry):
        first = index * GROUP
        left = by_row[pl.ds(first, GROUP)].reshape(GROUP * MAIN, LANE).astype(BF)
        mixed = dot(left, near[...])
        for batch in range(GROUP // BATCH):
            sides = []
            for side in range(BATCH):
                own = BATCH * batch + side
                sides.append(
                    jnp.concatenate(
                        [mixed[MAIN * own : MAIN * (own + 1), block(k)] for k in range(DD)]
                        + [rest[first + own], jnp.zeros((8, LANE), F32)],
                        axis=0,
                    ).astype(BF)
                )
            result = dot(arranged[...], jnp.concatenate(sides, axis=1))
            for pair in range(BATCH // 2):
                at = pl.multiple_of((first + BATCH * batch + 2 * pair) * MAIN, 16)
                for k in range(DD):
                    rows = slice(MAIN * k, MAIN * (k + 1))
                    pushed[k // 2, pl.ds(at, 2 * MAIN), block(k % 2)] = jnp.concatenate(
                        [result[rows, block(2 * pair)], result[rows, block(2 * pair + 1)]], axis=0
                    ).astype(BF)
            for side in range(BATCH):
                rest[first + BATCH * batch + side] = result[
                    MAIN * DD : MAIN * DD + 32, block(side)
                ]
        return carry

    lax.fori_loop(0, CHI // GROUP, group, 0)
    for k in range(DD):
        pushed[k // 2, CHI * MAIN : CHI * MAIN + ROWS, block(k % 2)] = jnp.concatenate(
            [rest[:, k, :], jnp.zeros((8, LANE), F32)], axis=0
        ).astype(BF)


def close(far, pushed, edge):
    def one(pair, total):
        value = dot(far[...], pushed[pair])
        edge[pair] = value
        return total + jnp.sum(value * value)

    total = lax.fori_loop(0, PAIRS, one, jnp.zeros((), F32))
    return jnp.sqrt(total / (CHI * DD * CHI) + 1e-06)


def narrow(edge, scale, dense, wide=None):
    for k in range(DD):
        value = (edge[k // 2, :, block(k % 2)] / scale).astype(BF)
        if wide is not None:
            wide[0:ROWS, block(k)] = value
        dense[:, CHI * k : CHI * (k + 1)] = value[0:CHI, 0:CHI]


def kernel(
    c1, c2, c4, t1, t2, t3, t4, tensors, pattern, s_below, s_above, s_right, s_left,
    o_left_top, o_left_edge, o_left_bottom, o_top_left, o_top_edge, o_top_right,
    c1_next, t1_next, far_left, far_top, corner_in,
    wide_a, wide_b, wide_c, wide_d, wide_e, wide_t, square_a, square_b,
    by_row, rest, pushed, edge, cholesky, turned, turned_top, dense, dense_top,
    corner_out, site_tensors, slices, packed, a_left, a_top, fetched, send, receive,
):
    col, row = lax.axis_index("col"), lax.axis_index("row")
    columns, rows = lax.axis_size("col"), lax.axis_size("row")
    right, left = lax.rem(col + 1, columns), lax.rem(col + columns - 1, columns)
    below, above = lax.rem(row + 1, rows), lax.rem(row + rows - 1, rows)
    to_above, to_below = (col, above), (col, below)
    to_right, to_diagonal = (right, row), (right, below)
    fetch = pltpu.make_async_copy(tensors, site_tensors, fetched)
    fetch.start()
    barrier = pltpu.get_barrier_semaphore()
    for device in (to_above, to_below, to_right, (left, row), to_diagonal, (left, above)):
        pl.semaphore_signal(barrier, inc=1, device_id=device, device_id_type=MESH)
    pl.semaphore_wait(barrier, 6)

    def ship(source, target, index, device):
        copy = pltpu.make_async_remote_copy(
            src_ref=source, dst_ref=target, send_sem=send.at[index],
            recv_sem=receive.at[index], device_id=device, device_id_type=MESH,
        )
        copy.start()
        return copy

    get_t1 = ship(t1, t1_next, 0, to_above)
    get_c1 = ship(c1, c1_next, 1, to_above)

    for ref in (wide_a, wide_b, wide_c, wide_d, wide_e):
        ref[...] = jnp.zeros_like(ref)
    rest[...] = jnp.zeros_like(rest)
    for pair in range(PAIRS):
        pushed[pair, CHI * MAIN + ROWS :, :] = jnp.zeros(
            (DEPTH - CHI * MAIN - ROWS, 2 * LANE), BF
        )
    pushed[PAIRS - 1, :, LANE:] = jnp.zeros((DEPTH, LANE), BF)
    for ref in (turned, turned_top):
        ref[:, CHI * MAIN + ROWS :] = jnp.zeros((ROWS, DEPTH - CHI * MAIN - ROWS), BF)
    widen(t2, wide_t)
    pad_square(c2, square_a)
    wide_d[0:ROWS, :] = dot(square_a[0:ROWS], wide_t[...]).astype(BF)
    widen(t3, wide_t)
    pad_square(c4, square_a)
    wide_b[0:ROWS, :] = dot(square_a[0:ROWS], wide_t[...]).astype(BF)

    def sketch_pair(sketch):
        pad_square_f32 = square_b
        pad_square_f32[...] = jnp.zeros_like(square_b)
        pad_square_f32[0:CHI, 0:CHI] = sketch[...]
        return jnp.concatenate(split(square_b[...]), axis=1)

    below_pair = sketch_pair(s_below)
    above_pair = sketch_pair(s_above)
    fetch.wait()
    arrange(site_tensors, pattern[0, 0], slices, packed, a_left, a_top)
    get_t1.wait()
    get_c1.wait()
    widen(t1_next, wide_t)
    pad_square(c1_next, square_a)
    wide_c[0:ROWS, :] = dot(square_a[0:ROWS], wide_t[...]).astype(BF)
    for k in range(DD):
        joint = dot(wide_b[0:ROWS, block(k)], below_pair) + dot(
            wide_c[0:ROWS, block(k)], above_pair
        )
        wide_a[0:ROWS, block(k)] = (joint[:, 0:LANE] + joint[:, LANE:]).astype(BF)
    bottom, top = frame_of(wide_a, (wide_b, wide_c), cholesky, wide_e, by_row, turned)
    corner_out[0] = rms(bottom)[0:CHI, 0:CHI].astype(BF)
    corner_out[1] = rms(top)[0:CHI, 0:CHI].astype(BF)
    get_far = ship(turned, far_left, 2, to_below)
    get_corner = ship(corner_out.at[1], corner_in, 3, to_below)
    put_bottom = ship(corner_out.at[0], o_left_bottom, 4, to_right)
    put_top = ship(corner_out.at[1], o_left_top, 5, to_diagonal)
    widen(t4, wide_t)
    spread(wide_t, by_row)
    absorb(by_row, wide_t, wide_e, a_left, rest, pushed)
    get_far.wait()
    scale = close(far_left, pushed, edge)
    narrow(edge, scale, dense, wide_c)
    put_edge = ship(dense, o_left_edge, 6, to_right)
    get_corner.wait()
    square_b[...] = jnp.zeros_like(square_b)
    square_b[0:CHI, 0:CHI] = corner_in[...].astype(F32)
    wide_b[0:ROWS, :] = dot(square_b[...].T[0:ROWS].astype(BF), wide_c[...]).astype(BF)
    right_pair = sketch_pair(s_right)
    left_pair = sketch_pair(s_left)
    for k in range(DD):
        joint = dot(wide_d[0:ROWS, block(k)], right_pair) + dot(
            wide_b[0:ROWS, block(k)], left_pair
        )
        wide_a[0:ROWS, block(k)] = (joint[:, 0:LANE] + joint[:, LANE:]).astype(BF)
    side, head = frame_of(wide_a, (wide_d, wide_b), cholesky, wide_e, by_row, turned_top)
    corner_out[2] = rms(side)[0:CHI, 0:CHI].astype(BF)
    corner_out[3] = rms(head).T[0:CHI, 0:CHI].astype(BF)
    get_far_top = ship(turned_top, far_top, 7, to_right)
    put_side = ship(corner_out.at[2], o_top_right, 8, to_below)
    put_head = ship(corner_out.at[3], o_top_left, 9, to_diagonal)
    widen(t1, wide_t)
    spread(wide_t, by_row)
    absorb(by_row, wide_t, wide_e, a_top, rest, pushed)
    get_far_top.wait()
    scale = close(far_top, pushed, edge)
    narrow(edge, scale, dense_top)
    put_top_edge = ship(dense_top, o_top_edge, 10, to_below)
    for copy in (put_bottom, put_top, put_edge, put_side, put_head, put_top_edge):
        copy.wait()


def arrange(tensors, index, slices, packed, a_left, a_top):
    count = tensors.shape[1]
    place = lax.broadcasted_iota(jnp.int32, (32, count * DD), 0) * count + index
    entry = lax.broadcasted_iota(jnp.int32, (32, count * DD), 1)
    pick = jnp.where(entry == place, 1.0, 0.0).astype(BF)
    for i in range(DD):
        several = tensors[DD * i : DD * (i + 1)].reshape(count * DD, DD * DD)
        rows = jnp.concatenate(
            [dot(pick, several), jnp.zeros((32, SQUARE - DD * DD), F32)], axis=1
        )
        slices[i] = rows.T
    margin = SQUARE - DD * DD

    def gather(kr, carry):
        pieces = [slices[0:MAIN, DD * kd + kr, 0:DD] for kd in range(DD)]
        packed[pl.ds(pl.multiple_of(kr * MAIN, 8), MAIN), :] = jnp.concatenate(
            pieces + [jnp.zeros((MAIN, margin), F32)], axis=1
        )
        return carry

    lax.fori_loop(0, DD, gather, 0)
    pieces = [slices[MAIN, DD * kd : DD * (kd + 1), 0:DD] for kd in range(DD)]
    last = jnp.concatenate(pieces + [jnp.zeros((DD, margin), F32)], axis=1)
    packed[DD * MAIN :, :] = jnp.concatenate(
        [last, jnp.zeros((SQUARE - DD * DD, SQUARE), F32)], axis=0
    )
    source = lax.broadcasted_iota(jnp.int32, (SQUARE, SQUARE), 0)
    target = lax.broadcasted_iota(jnp.int32, (1, SQUARE), 1)
    wanted = jnp.where(
        target < DD * MAIN,
        target + target // MAIN,
        jnp.where(target < DD * DD, (target - DD * MAIN) * DD + MAIN, -1),
    )
    choose = jnp.where(source == wanted, 1.0, 0.0).astype(BF)
    result = dot(packed[...].astype(BF), choose)
    a_left[...] = result.astype(BF)
    a_top[...] = result.T.astype(BF)


def hand_on(*refs):
    for source, target in zip(refs[:6], refs[6:]):
        target[...] = source[...]


def body(
    corner_top_left, corner_top_right, corner_bottom_left, edge_top, edge_right,
    edge_bottom, edge_left, tensors, pattern, sketch_below, sketch_above,
    sketch_right, sketch_left,
):
    corner = jax.ShapeDtypeStruct((CHI, CHI), BF)
    long = jax.ShapeDtypeStruct((CHI, DD * CHI), BF)
    vmem = pl.BlockSpec(memory_space=pltpu.VMEM)
    wide = pltpu.VMEM((LANE, WIDE), BF)
    by_leg = tensors.transpose(1, 0, 2)
    anywhere = pl.BlockSpec(memory_space=pl.ANY)
    shapes = (corner, long, corner, corner, long, corner)
    moved = pl.pallas_call(
        kernel,
        out_shape=shapes,
        in_specs=[vmem] * 7
        + [anywhere, pl.BlockSpec(memory_space=pltpu.SMEM)]
        + [vmem] * 4,
        out_specs=[anywhere] * 6,
        scratch_shapes=[
            pltpu.VMEM((CHI, CHI), BF),
            pltpu.VMEM((CHI, DD * CHI), BF),
            pltpu.VMEM((ROWS, DEPTH), BF),
            pltpu.VMEM((ROWS, DEPTH), BF),
            pltpu.VMEM((CHI, CHI), BF),
            wide, wide, wide, wide, wide, wide,
            pltpu.VMEM((LANE, LANE), BF),
            pltpu.VMEM((LANE, LANE), F32),
            pltpu.VMEM((CHI, MAIN, LANE), F32),
            pltpu.VMEM((104, 32, LANE), F32),
            pltpu.VMEM((PAIRS, DEPTH, 2 * LANE), BF),
            pltpu.VMEM((PAIRS, ROWS, 2 * LANE), F32),
            pltpu.VMEM((LANE, 2 * LANE), F32),
            pltpu.VMEM((ROWS, DEPTH), BF),
            pltpu.VMEM((ROWS, DEPTH), BF),
            pltpu.VMEM((CHI, DD * CHI), BF),
            pltpu.VMEM((CHI, DD * CHI), BF),
            pltpu.VMEM((4, CHI, CHI), BF),
            pltpu.VMEM(by_leg.shape, BF),
            pltpu.VMEM((DD, SQUARE, 32), F32),
            pltpu.VMEM((SQUARE, SQUARE), F32),
            pltpu.VMEM((SQUARE, SQUARE), BF),
            pltpu.VMEM((SQUARE, SQUARE), BF),
            pltpu.SemaphoreType.DMA(()),
            pltpu.SemaphoreType.DMA((11,)),
            pltpu.SemaphoreType.DMA((11,)),
        ],
        compiler_params=pltpu.CompilerParams(
            collective_id=0, has_side_effects=True, vmem_limit_bytes=60 * 1024 * 1024
        ),
    )(
        corner_top_left, corner_top_right, corner_bottom_left, edge_top, edge_right,
        edge_bottom, edge_left, by_leg, pattern, sketch_below, sketch_above,
        sketch_right, sketch_left,
    )
    return pl.pallas_call(
        hand_on,
        out_shape=shapes,
        in_specs=[vmem] * 6,
        out_specs=[vmem] * 6,
    )(*moved)


def solution(mesh):
    split_both = P("col", "row")
    in_specs = (split_both,) * 7 + (P(), split_both) + (P(),) * 4
    return jax.shard_map(
        body, mesh=mesh, in_specs=in_specs, out_specs=(split_both,) * 6, check_vma=False
    )
```

```python
import functools

import jax
import jax.numpy as jnp
from jax import lax
from jax.experimental import pallas as pl
from jax.experimental.pallas import tpu as pltpu
from jax.sharding import PartitionSpec as P

CHI = 100
DD = 25
LANE = 128
ROWS = 112
MAIN = DD - 1
WIDE = DD * LANE
SQUARE = 640
DEPTH = 2560
PAIRS = 13
GROUP = 20
BATCH = 10
LEAVING = (3, 7, 10, 12)
RUNS = (0, 768, 1536, 2176, DEPTH)
BF = jnp.bfloat16
F32 = jnp.float32
MESH = pl.DeviceIdType.MESH


def dot(a, b):
    return jnp.dot(a, b, preferred_element_type=F32)


def dot_exact(a, b):
    return lax.dot_general(
        a, b, (((1,), (0,)), ((), ())), precision=lax.Precision.HIGHEST,
        preferred_element_type=F32,
    )


def split(values):
    high = values.astype(BF)
    return high, (values - high.astype(F32)).astype(BF)


def block(k):
    return slice(LANE * k, LANE * (k + 1))


def widen(source, target):
    target[...] = jnp.zeros_like(target)
    for k in range(DD):
        target[0:CHI, LANE * k : LANE * k + CHI] = source[:, CHI * k : CHI * (k + 1)]


def pad_square(source, target):
    target[...] = jnp.zeros_like(target)
    target[0:CHI, 0:CHI] = source[...]


def rms(values):
    scale = jnp.sqrt(jnp.sum(values * values) / (CHI * CHI) + 1e-06)
    return values / scale


def factor_inverse(gram, work):
    rows = lax.broadcasted_iota(jnp.int32, (LANE, LANE), 0)
    columns = lax.broadcasted_iota(jnp.int32, (LANE, LANE), 1)
    eye = (rows == columns).astype(F32)
    work[:, 0:LANE] = gram
    work[:, LANE:] = eye
    inner = lax.broadcasted_iota(jnp.int32, (8, LANE), 0)
    for start in range(0, 104, 8):
        halves = [work[start : start + 8, block(n)] for n in range(2)]
        tall = [
            jnp.broadcast_to(halves[0][:, start + n : start + n + 1], (8, LANE)) for n in range(8)
        ]
        for step in range(8):
            if start + step >= CHI:
                break
            inverse = lax.rsqrt(jnp.broadcast_to(tall[step][step : step + 1], (8, LANE)))
            factor = tall[step] * inverse
            for later in range(step + 1, 8):
                tall[later] = tall[later] - factor * factor[later : later + 1]
            for n in range(2):
                row = halves[n][step : step + 1] * inverse
                halves[n] = jnp.where(
                    inner < step,
                    halves[n],
                    jnp.where(inner == step, row, halves[n] - factor * row),
                )
        panel = jnp.concatenate(halves, axis=1)
        work[start : start + 8, :] = panel
        if start + 8 < 104:
            high = panel.astype(BF).astype(F32)
            middle = (panel - high).astype(BF).astype(F32)
            low = panel - high - middle
            tall_parts = [part[:, :LANE] for part in (high, high, high, middle, middle, low)]
            update = lax.dot_general(
                jnp.concatenate(tall_parts, axis=0).T.astype(BF),
                jnp.concatenate([high, middle, low, high, middle, high], axis=0).astype(BF),
                (((1,), (0,)), ((), ())), preferred_element_type=F32,
            )
            work[start + 8 : 104, :] = work[start + 8 : 104, :] - update[start + 8 : 104, :]
    inverse = work[:, LANE:]
    return jnp.where((rows >= CHI) & (rows != columns), 0.0, inverse)


def frame_of(sketched, others, cholesky, wide_frame, by_row, turned):
    count = len(others) + 1
    total = jnp.zeros((LANE, count * LANE), F32)
    for k in range(DD):
        own = sketched[:, block(k)]
        right = jnp.concatenate([own] + [other[:, block(k)] for other in others], axis=1)
        total = total + lax.dot_general(
            own, right, (((0,), (0,)), ((), ())), preferred_element_type=F32
        )
    rows = lax.broadcasted_iota(jnp.int32, (LANE, LANE), 0)
    columns = lax.broadcasted_iota(jnp.int32, (LANE, LANE), 1)
    gram = jnp.where((rows == columns) & (rows >= CHI), 1.0, total[:, 0:LANE])
    inverse = factor_inverse(gram, cholesky)
    products = [dot_exact(inverse, total[:, block(1 + n)]) for n in range(len(others))]
    high, low = split(inverse)
    both = jnp.concatenate([high, low], axis=0)
    for k in range(DD):
        joint = lax.dot_general(
            sketched[0:ROWS, block(k)], both, (((1,), (1,)), ((), ())),
            preferred_element_type=F32,
        )
        frame = joint[:, 0:LANE] + joint[:, LANE:]
        wide_frame[0:ROWS, block(k)] = frame.astype(BF)
        if k < MAIN:
            by_row[:, k, :] = frame[0:CHI]
        else:
            turned[:, CHI * MAIN : CHI * MAIN + ROWS] = frame.T[0:ROWS].astype(BF)
    flat = by_row[...].reshape(CHI * MAIN, LANE)
    turned[:, 0 : CHI * MAIN] = flat.T[0:ROWS].astype(BF)
    return products


def spread(edge_wide, by_row):
    for j in range(MAIN):
        by_row[:, j, :] = edge_wide[0:CHI, block(j)].astype(F32)


def absorb(by_row, edge_wide, near, arranged, rest, pushed):
    last = dot(edge_wide[0:ROWS, block(MAIN)], near[...])
    for k in range(DD):
        rest[:, k, :] = last[0:104, block(k)]

    def group(index, carry):
        first = index * GROUP
        left = by_row[pl.ds(first, GROUP)].reshape(GROUP * MAIN, LANE).astype(BF)
        mixed = dot(left, near[...])
        for batch in range(GROUP // BATCH):
            sides = []
            for side in range(2):
                pieces = []
                for entry in range(BATCH // 2):
                    own = BATCH * batch + 2 * entry + side
                    pieces.append(
                        jnp.concatenate(
                            [mixed[MAIN * own : MAIN * (own + 1), block(k)] for k in range(DD)]
                            + [rest[first + own], jnp.zeros((8, LANE), F32)],
                            axis=0,
                        ).astype(BF)[:, 0:CHI]
                    )
                pieces.append(jnp.zeros((SQUARE, 4 * LANE - 5 * CHI), BF))
                sides.append(jnp.concatenate(pieces, axis=1))
            result = dot(arranged[...], jnp.concatenate(sides, axis=1))
            for entry in range(BATCH // 2):
                at = pl.multiple_of((first + BATCH * batch + 2 * entry) * MAIN, 16)
                low = CHI * entry // LANE * LANE
                high = -(-CHI * (entry + 1) // LANE) * LANE
                offset = CHI * entry - low
                margin = jnp.zeros((2 * MAIN, LANE - CHI), BF)
                for k in range(DD):
                    rows = slice(MAIN * k, MAIN * (k + 1))
                    both = jnp.concatenate(
                        [result[rows, low:high], result[rows, 4 * LANE + low : 4 * LANE + high]],
                        axis=0,
                    ).astype(BF)
                    pushed[k // 2, pl.ds(at, 2 * MAIN), block(k % 2)] = jnp.concatenate(
                        [both[:, offset : offset + CHI], margin], axis=1
                    )
                for side in range(2):
                    from_lane = 4 * LANE * side + CHI * entry
                    rest[first + BATCH * batch + 2 * entry + side, :, 0:CHI] = result[
                        MAIN * DD : MAIN * DD + 32, from_lane : from_lane + CHI
                    ]
        return carry

    lax.fori_loop(0, CHI // GROUP, group, 0)
    for k in range(DD):
        pushed[k // 2, CHI * MAIN : CHI * MAIN + ROWS, block(k % 2)] = jnp.concatenate(
            [rest[:, k, :], jnp.zeros((8, LANE), F32)], axis=0
        ).astype(BF)


def squares(values):
    return jnp.sum((values * values).reshape(ROWS // 8, 8, 2 * LANE), axis=0)


def inverse_scale(total):
    return lax.rsqrt(jnp.sum(total) / (CHI * DD * CHI) + 1e-06)


def close(far, pushed, edge):
    total = jnp.zeros((8, 2 * LANE), F32)
    for pair in range(PAIRS):
        value = dot(far[...], pushed[pair])
        edge[pair] = value
        total = total + squares(value)
    return inverse_scale(total)


def close_out(far, pushed, dense, leave):
    total = jnp.zeros((8, 2 * LANE), F32)
    for pair in range(PAIRS):
        value = dot(far[...], pushed[pair])
        total = total + squares(value)
        for side in range(2):
            k = 2 * pair + side
            if k < DD:
                dense[:, CHI * k : CHI * (k + 1)] = value[
                    :, LANE * side : LANE * side + CHI
                ].astype(BF)
        if pair in LEAVING:
            leave(LEAVING.index(pair))
    return inverse_scale(total)


def narrow(edge, scale, dense, wide):
    for k in range(DD):
        value = (edge[k // 2, :, block(k % 2)] * scale).astype(BF)
        wide[0:ROWS, block(k)] = value
        dense[:, CHI * k : CHI * (k + 1)] = value[0:CHI, 0:CHI]


def kernel(
    c1, c2, c4, t1, t2, t3, t4, tensors, pattern, s_below, s_above, s_right, s_left,
    o_left_top, o_left_edge, o_left_bottom, o_top_left, o_top_edge, o_top_right, o_top_scale,
    c1_next, t1_next, far_left, far_top, corner_in,
    wide_a, wide_b, wide_c, wide_d, wide_e, wide_t, square_a, square_b,
    by_row, rest, pushed, edge, cholesky, turned, turned_top, dense, dense_top,
    corner_out, scale_out, site_tensors, slices, packed, a_left, a_top, fetched, send, receive,
):
    col, row = lax.axis_index("col"), lax.axis_index("row")
    columns, rows = lax.axis_size("col"), lax.axis_size("row")
    right, left = lax.rem(col + 1, columns), lax.rem(col + columns - 1, columns)
    below, above = lax.rem(row + 1, rows), lax.rem(row + rows - 1, rows)
    to_above, to_below = (col, above), (col, below)
    to_right, to_diagonal = (right, row), (right, below)
    fetch = pltpu.make_async_copy(tensors, site_tensors, fetched)
    fetch.start()
    barrier = pltpu.get_barrier_semaphore()
    for device in (to_above, to_below, to_right, (left, row), to_diagonal, (left, above)):
        pl.semaphore_signal(barrier, inc=1, device_id=device, device_id_type=MESH)
    pl.semaphore_wait(barrier, 6)

    def ship(source, target, index, device):
        copy = pltpu.make_async_remote_copy(
            src_ref=source, dst_ref=target, send_sem=send.at[index],
            recv_sem=receive.at[index], device_id=device, device_id_type=MESH,
        )
        copy.start()
        return copy

    get_t1 = ship(t1, t1_next, 0, to_above)
    get_c1 = ship(c1, c1_next, 1, to_above)

    for ref in (wide_a, wide_b, wide_c, wide_d, wide_e):
        ref[...] = jnp.zeros_like(ref)
    rest[...] = jnp.zeros_like(rest)
    for pair in range(PAIRS):
        pushed[pair, CHI * MAIN + ROWS :, :] = jnp.zeros(
            (DEPTH - CHI * MAIN - ROWS, 2 * LANE), BF
        )
    pushed[PAIRS - 1, :, LANE:] = jnp.zeros((DEPTH, LANE), BF)
    dense_top[:, CHI * DD :] = jnp.zeros((ROWS, DEPTH - CHI * DD), BF)
    for ref in (turned, turned_top):
        ref[:, CHI * MAIN + ROWS :] = jnp.zeros((ROWS, DEPTH - CHI * MAIN - ROWS), BF)
    widen(t2, wide_t)
    pad_square(c2, square_a)
    wide_d[0:ROWS, :] = dot(square_a[0:ROWS], wide_t[...]).astype(BF)
    widen(t3, wide_t)
    pad_square(c4, square_a)
    wide_b[0:ROWS, :] = dot(square_a[0:ROWS], wide_t[...]).astype(BF)

    def sketch_pair(sketch):
        pad_square_f32 = square_b
        pad_square_f32[...] = jnp.zeros_like(square_b)
        pad_square_f32[0:CHI, 0:CHI] = sketch[...]
        return jnp.concatenate(split(square_b[...]), axis=1)

    below_pair = sketch_pair(s_below)
    above_pair = sketch_pair(s_above)
    fetch.wait()
    arrange(site_tensors, pattern[0, 0], slices, packed, a_left, a_top)
    get_t1.wait()
    get_c1.wait()
    widen(t1_next, wide_t)
    pad_square(c1_next, square_a)
    wide_c[0:ROWS, :] = dot(square_a[0:ROWS], wide_t[...]).astype(BF)
    for k in range(DD):
        joint = dot(wide_b[0:ROWS, block(k)], below_pair) + dot(
            wide_c[0:ROWS, block(k)], above_pair
        )
        wide_a[0:ROWS, block(k)] = (joint[:, 0:LANE] + joint[:, LANE:]).astype(BF)
    bottom, top = frame_of(wide_a, (wide_b, wide_c), cholesky, wide_e, by_row, turned)
    corner_out[0] = rms(bottom)[0:CHI, 0:CHI].astype(BF)
    corner_out[1] = rms(top)[0:CHI, 0:CHI].astype(BF)
    get_far = ship(turned, far_left, 2, to_below)
    get_corner = ship(corner_out.at[1], corner_in, 3, to_below)
    put_bottom = ship(corner_out.at[0], o_left_bottom, 4, to_right)
    put_top = ship(corner_out.at[1], o_left_top, 5, to_diagonal)
    widen(t4, wide_t)
    spread(wide_t, by_row)
    absorb(by_row, wide_t, wide_e, a_left, rest, pushed)
    get_far.wait()
    scale = close(far_left, pushed, edge)
    narrow(edge, scale, dense, wide_c)
    put_edge = ship(dense, o_left_edge, 6, to_right)
    get_corner.wait()
    square_b[...] = jnp.zeros_like(square_b)
    square_b[0:CHI, 0:CHI] = corner_in[...].astype(F32)
    wide_b[0:ROWS, :] = dot(square_b[...].T[0:ROWS].astype(BF), wide_c[...]).astype(BF)
    right_pair = sketch_pair(s_right)
    left_pair = sketch_pair(s_left)
    for k in range(DD):
        joint = dot(wide_d[0:ROWS, block(k)], right_pair) + dot(
            wide_b[0:ROWS, block(k)], left_pair
        )
        wide_a[0:ROWS, block(k)] = (joint[:, 0:LANE] + joint[:, LANE:]).astype(BF)
    side, head = frame_of(wide_a, (wide_d, wide_b), cholesky, wide_e, by_row, turned_top)
    corner_out[2] = rms(side)[0:CHI, 0:CHI].astype(BF)
    corner_out[3] = rms(head).T[0:CHI, 0:CHI].astype(BF)
    get_far_top = ship(turned_top, far_top, 7, to_right)
    put_side = ship(corner_out.at[2], o_top_right, 8, to_below)
    put_head = ship(corner_out.at[3], o_top_left, 9, to_diagonal)
    widen(t1, wide_t)
    spread(wide_t, by_row)
    absorb(by_row, wide_t, wide_e, a_top, rest, pushed)
    get_far_top.wait()
    leaving = []

    def leave(run):
        columns = pl.ds(RUNS[run], RUNS[run + 1] - RUNS[run])
        leaving.append(
            ship(dense_top.at[:, columns], o_top_edge.at[:, columns], 10 + run, to_below)
        )

    scale_out[...] = jnp.broadcast_to(
        close_out(far_top, pushed, dense_top, leave), scale_out.shape
    )
    put_scale = ship(scale_out, o_top_scale, 14, to_below)
    for copy in (put_bottom, put_top, put_edge, put_side, put_head, *leaving, put_scale):
        copy.wait()


def arrange(tensors, index, slices, packed, a_left, a_top):
    count = tensors.shape[1]
    place = lax.broadcasted_iota(jnp.int32, (32, count * DD), 0) * count + index
    entry = lax.broadcasted_iota(jnp.int32, (32, count * DD), 1)
    pick = jnp.where(entry == place, 1.0, 0.0).astype(BF)
    blank = jnp.zeros((32, SQUARE), F32)

    def of(i):
        several = tensors[DD * i : DD * (i + 1)].reshape(count * DD, DD * DD)
        return jnp.concatenate(
            [dot(pick, several), jnp.zeros((32, SQUARE - DD * DD), F32)], axis=1
        )

    for i in range(8):
        after = of(MAIN) if i == 0 else blank
        slices[i] = jnp.concatenate([of(i), of(i + 8), of(i + 16), after], axis=0).T
    margin = SQUARE - DD * DD

    def gather(kr, carry):
        loaded = [slices[:, DD * kd + kr, :] for kd in range(DD)]
        rows = []
        for third in range(3):
            pieces = [each[:, 32 * third : 32 * third + DD] for each in loaded]
            rows.append(jnp.concatenate(pieces + [jnp.zeros((8, margin), F32)], axis=1))
        packed[pl.ds(pl.multiple_of(kr * MAIN, 8), MAIN), :] = jnp.concatenate(rows, axis=0)
        return carry

    lax.fori_loop(0, DD, gather, 0)
    pieces = [slices[0, DD * kd : DD * (kd + 1), 96 : 96 + DD] for kd in range(DD)]
    last = jnp.concatenate(pieces + [jnp.zeros((DD, margin), F32)], axis=1)
    packed[DD * MAIN :, :] = jnp.concatenate(
        [last, jnp.zeros((SQUARE - DD * DD, SQUARE), F32)], axis=0
    )
    source = lax.broadcasted_iota(jnp.int32, (SQUARE, SQUARE), 0)
    target = lax.broadcasted_iota(jnp.int32, (1, SQUARE), 1)
    wanted = jnp.where(
        target < DD * MAIN,
        target + target // MAIN,
        jnp.where(target < DD * DD, (target - DD * MAIN) * DD + MAIN, -1),
    )
    choose = jnp.where(source == wanted, 1.0, 0.0).astype(BF)
    result = dot(packed[...].astype(BF), choose)
    a_left[...] = result.astype(BF)
    a_top[...] = result.T.astype(BF)


def hand_on(*refs):
    scale = refs[6][0:1, 0:1]
    for n, (source, target) in enumerate(zip(refs[:6], refs[7:])):
        if n == 4:
            target[...] = (source[0:CHI, 0 : CHI * DD].astype(F32) * scale).astype(BF)
        else:
            target[...] = source[...]


def body(
    corner_top_left, corner_top_right, corner_bottom_left, edge_top, edge_right,
    edge_bottom, edge_left, tensors, pattern, sketch_below, sketch_above,
    sketch_right, sketch_left,
):
    corner = jax.ShapeDtypeStruct((CHI, CHI), BF)
    long = jax.ShapeDtypeStruct((CHI, DD * CHI), BF)
    vmem = pl.BlockSpec(memory_space=pltpu.VMEM)
    wide = pltpu.VMEM((LANE, WIDE), BF)
    by_leg = tensors.transpose(1, 0, 2)
    anywhere = pl.BlockSpec(memory_space=pl.ANY)
    raw = jax.ShapeDtypeStruct((ROWS, DEPTH), BF)
    scale = jax.ShapeDtypeStruct((8, LANE), F32)
    shapes = (corner, long, corner, corner, long, corner)
    moved = pl.pallas_call(
        kernel,
        out_shape=(*shapes[:4], raw, corner, scale),
        in_specs=[vmem] * 7
        + [anywhere, pl.BlockSpec(memory_space=pltpu.SMEM)]
        + [vmem] * 4,
        out_specs=[anywhere] * 7,
        scratch_shapes=[
            pltpu.VMEM((CHI, CHI), BF),
            pltpu.VMEM((CHI, DD * CHI), BF),
            pltpu.VMEM((ROWS, DEPTH), BF),
            pltpu.VMEM((ROWS, DEPTH), BF),
            pltpu.VMEM((CHI, CHI), BF),
            wide, wide, wide, wide, wide, wide,
            pltpu.VMEM((LANE, LANE), BF),
            pltpu.VMEM((LANE, LANE), F32),
            pltpu.VMEM((CHI, MAIN, LANE), F32),
            pltpu.VMEM((104, 32, LANE), F32),
            pltpu.VMEM((PAIRS, DEPTH, 2 * LANE), BF),
            pltpu.VMEM((PAIRS, ROWS, 2 * LANE), F32),
            pltpu.VMEM((LANE, 2 * LANE), F32),
            pltpu.VMEM((ROWS, DEPTH), BF),
            pltpu.VMEM((ROWS, DEPTH), BF),
            pltpu.VMEM((CHI, DD * CHI), BF),
            pltpu.VMEM((ROWS, DEPTH), BF),
            pltpu.VMEM((4, CHI, CHI), BF),
            pltpu.VMEM((8, LANE), F32),
            pltpu.VMEM(by_leg.shape, BF),
            pltpu.VMEM((8, SQUARE, LANE), F32),
            pltpu.VMEM((SQUARE, SQUARE), F32),
            pltpu.VMEM((SQUARE, SQUARE), BF),
            pltpu.VMEM((SQUARE, SQUARE), BF),
            pltpu.SemaphoreType.DMA(()),
            pltpu.SemaphoreType.DMA((15,)),
            pltpu.SemaphoreType.DMA((15,)),
        ],
        compiler_params=pltpu.CompilerParams(
            collective_id=0, has_side_effects=True, vmem_limit_bytes=60 * 1024 * 1024
        ),
    )(
        corner_top_left, corner_top_right, corner_bottom_left, edge_top, edge_right,
        edge_bottom, edge_left, by_leg, pattern, sketch_below, sketch_above,
        sketch_right, sketch_left,
    )
    return pl.pallas_call(
        hand_on,
        out_shape=shapes,
        in_specs=[vmem] * 7,
        out_specs=[vmem] * 6,
    )(*moved)


def solution(mesh):
    split_both = P("col", "row")
    in_specs = (split_both,) * 7 + (P(), split_both) + (P(),) * 4
    return jax.shard_map(
        body, mesh=mesh, in_specs=in_specs, out_specs=(split_both,) * 6, check_vma=False
    )
```
